32 devices in a mesh: groups: 2 (over y), wide: 4 (over x, core), tok: 4 (over z).
Axes of the slice: x: 2, y: 2, z: 4, core: 2. Of those that a mesh axis runs over, the one named last changes fastest.
Arguments:
- acts: bfloat16 [256, 8192], P(('groups', 'wide'), 'tok'), parts along dimension 0, may hold values from -6 to 6
- cotangent: bfloat16 [256, 8192], P(('groups', 'wide'), 'tok'), parts along dimension 0, may hold values from -6 to 6
- gate_weight: bfloat16 [8192, 14336], P('tok', 'wide'), may hold values from -0.0625 to 0.0625
- up_weight: bfloat16 [8192, 14336], P('tok', 'wide'), may hold values from -0.0625 to 0.0625
- down_weight: bfloat16 [14336, 8192], P('wide', 'tok'), may hold values from -0.046875 to 0.046875
- block_lists: int32 [3, 112, 4, 16], P(None, 'wide', 'tok'), may hold values from 0 to 15, as said below
- block_counts: int32 [3, 112, 4], P(None, 'wide', 'tok'), may hold values from 0 to 16, as said below
- decay: float32 [3], replicated, may hold values from 100 to 1000
Outputs:
- layer_out: bfloat16 [256, 8192], P(('groups', 'wide'), 'tok'), parts along dimension 0
- input_grad: bfloat16 [256, 8192], P(('groups', 'wide'), 'tok'), parts along dimension 0
- gate_grad: bfloat16 [16384, 14336], P(('groups', 'tok'), 'wide'), parts along dimension 0
- up_grad: bfloat16 [16384, 14336], P(('groups', 'tok'), 'wide'), parts along dimension 0
- down_grad: bfloat16 [28672, 8192], P(('groups', 'wide'), 'tok'), parts along dimension 0
The draws below stay inside these ranges and needn't reach their ends.
There are 2 independent parts, one for each index of `groups`. The reference program is written for one: setup_inputs(seed, part) draws one part's arguments, and reference() takes and returns one part's arrays. A program takes and returns all parts, laid end to end along the dimension named above; an argument that names none is the same for every part. Nothing has to cross between parts.
Inputs may be any that keep to these rules, and one draw needn't show every extreme that they name: `block_lists`: for each projection, hidden-unit block and index of tok, the row is an ordering of the 16 local model-width block numbers: its first block_counts entries are the kept blocks in ascending order, the rest the pruned blocks in ascending order. `block_counts`: for each projection and hidden-unit block, exactly half of the 64 model-width blocks are kept in all, and one index of tok keeps all of its blocks.
All inputs are finite; a program needn't handle non-finite values.
Results may differ from the reference program's by a relative error of at most 0.02.
Values may be sent and summed in bfloat16 or wider, within the bound.
A program may use at most 256 MiB of HBM per device.

```python
import math
import jax
import jax.numpy as jnp
from jax import lax

D = 8192
FF = 14336
BLK = 128
TOKENS = 128
N_WIDE = 4
N_TOK = 4


def block_pattern(key):
    key = jax.random.fold_in(key, 11)
    total_blocks = D // BLK
    half = total_blocks // 2
    per_device = D // (N_TOK * BLK)
    columns = FF // BLK

    def one_column(column_key):
        first_key, second_key = jax.random.split(column_key)
        full_owner = jax.random.randint(first_key, (), 0, N_TOK)
        order = jax.random.permutation(second_key, total_blocks)
        rank = jnp.argsort(order, stable=True).astype(jnp.int32)
        blocks = jnp.arange(total_blocks, dtype=jnp.int32)
        owner = blocks // per_device
        score = jnp.where(owner == full_owner, blocks - total_blocks, rank)
        sorted_ids = jnp.argsort(score, stable=True)
        ranks = jnp.argsort(sorted_ids, stable=True)
        return ranks < half
    keys = jax.random.split(key, 3 * columns)
    kept = jax.vmap(one_column)(keys).reshape(3, columns, N_TOK, per_device)
    local = jnp.arange(per_device, dtype=jnp.int32)
    counts = jnp.sum(kept.astype(jnp.int32), axis=-1).astype(jnp.int32)
    ordering = jnp.where(kept, 0, per_device).astype(jnp.int32) + local
    lists = jnp.argsort(ordering, axis=-1, stable=True).astype(jnp.int32)
    return (lists, counts)


def draw_block_lists(key, part):
    lists, counts = block_pattern(key)
    return lists


def draw_block_counts(key, part):
    lists, counts = block_pattern(key)
    return counts


def block_scale(own_key, dims, pieces, least, high):
    level, own = 1.0, jax.random.fold_in(own_key, 6)
    for dim, blocks in pieces:
        steps = jnp.exp(jax.random.uniform(jax.random.fold_in(own, dim), (blocks,), jnp.float32, least / len(pieces), high / len(pieces)))
        level = level * jnp.repeat(steps, dims[dim] // blocks).reshape([-1 if axis == dim else 1 for axis in range(len(dims))])
    return level


def centred(key, extent, deviation, most, shards=(), kind=jnp.bfloat16):
    entries = jax.random.normal(key, extent, jnp.float32) * deviation
    if len(shards) > 0:
        entries = block_scale(key, extent, shards, -0.22, 0.18) * entries
    return jnp.clip(entries, min=-most, max=most).astype(kind)


def setup_inputs(seed: int = 0, part: int = 0) -> dict:
    streams_of = jax.random.split(jax.random.key(seed), 9)
    part_splits = jax.random.split(jax.random.fold_in(streams_of[8], part), 9)
    return {
        "acts": centred(part_splits[0], (TOKENS, D), 1.0, 6.0, ((0, 4), (1, 4))),
        "cotangent": centred(part_splits[1], (TOKENS, D), 1.0, 6.0, ((0, 4), (1, 4))),
        "gate_weight": centred(streams_of[2], (D, FF), D ** -0.5, 0.0625, ((0, 4), (1, 4))),
        "up_weight": centred(streams_of[3], (D, FF), D ** -0.5, 0.0625, ((0, 4), (1, 4))),
        "down_weight": centred(streams_of[4], (FF, D), FF ** -0.5, 0.046875, ((0, 4), (1, 4))),
        "block_lists": draw_block_lists(jax.random.fold_in(streams_of[8], 71), part),
        "block_counts": draw_block_counts(jax.random.fold_in(streams_of[8], 71), part),
        "decay": jnp.clip(jnp.exp(jax.random.uniform(streams_of[7], (3,), jnp.float32, math.log(100.0), math.log(1000.0))), 100.0, 1000.0),
    }


def kept_blocks(block_lists, block_counts):
    per_device = D // (N_TOK * BLK)
    position = jnp.arange(per_device, dtype=jnp.int32)
    live = position < block_counts[..., None]
    hits = (block_lists[..., None] == position) & live[..., None]
    kept = jnp.any(hits, axis=-2)
    kept = kept.reshape(3, FF // BLK, D // BLK)
    return jnp.transpose(kept, (0, 2, 1))


def expand(blocks):
    return jnp.repeat(jnp.repeat(blocks.astype(jnp.bfloat16), BLK, 0), BLK, 1)


def split_sums(lhs, rhs):
    width = D // N_TOK

    def step(running, index):
        left = lax.dynamic_slice_in_dim(lhs, index * width, width, 1)
        right = lax.dynamic_slice_in_dim(rhs, index * width, width, 0)
        part = jnp.dot(left, right, preferred_element_type=jnp.float32).astype(jnp.bfloat16)
        part = lax.optimization_barrier(part)
        return running + part.astype(jnp.float32), None

    start = jnp.zeros((lhs.shape[0], rhs.shape[1]), jnp.float32)
    result, _ = lax.scan(step, start, jnp.arange(N_TOK, dtype=jnp.int32))
    return result


def wide_sums(lefts, rights):
    width = FF // N_WIDE

    def step(running, index):
        part = jnp.zeros((lefts[0].shape[0], rights[0].shape[1]), jnp.float32)
        for left_full, right_full in zip(lefts, rights):
            left = lax.dynamic_slice_in_dim(left_full, index * width, width, 1)
            right = lax.dynamic_slice_in_dim(right_full, index * width, width, 0)
            part = part + jnp.dot(left, right, preferred_element_type=jnp.float32)
        part = lax.optimization_barrier(part.astype(jnp.bfloat16))
        return running + part.astype(jnp.float32), None

    start = jnp.zeros((lefts[0].shape[0], rights[0].shape[1]), jnp.float32)
    result, _ = lax.scan(step, start, jnp.arange(N_WIDE, dtype=jnp.int32))
    return result


def reference(acts, cotangent, gate_weight, up_weight, down_weight, block_lists, block_counts, decay):
    kept = kept_blocks(block_lists, block_counts)
    mask_gate = expand(kept[0])
    mask_up = expand(kept[1])
    mask_down = expand(kept[2]).T
    gate_masked = gate_weight * mask_gate
    up_masked = up_weight * mask_up
    down_masked = down_weight * mask_down
    gate = split_sums(acts, gate_masked)
    up = split_sums(acts, up_masked)
    grad_hidden = split_sums(cotangent, down_masked.T)
    sigma = jax.nn.sigmoid(gate)
    silu = gate * sigma
    hidden = (silu * up).astype(jnp.bfloat16)
    gate_cot = (grad_hidden * up * sigma * (1.0 + gate * (1.0 - sigma))).astype(jnp.bfloat16)
    up_cot = (grad_hidden * silu).astype(jnp.bfloat16)
    layer_out = wide_sums((hidden,), (down_masked,)).astype(jnp.bfloat16)
    input_grad = wide_sums((gate_cot, up_cot), (gate_masked.T, up_masked.T)).astype(jnp.bfloat16)
    gate_grad = (jnp.dot(acts.T, gate_cot, preferred_element_type=jnp.float32)
                 + decay[0] * (1.0 - mask_gate.astype(jnp.float32)) * gate_weight.astype(jnp.float32)).astype(jnp.bfloat16)
    up_grad = (jnp.dot(acts.T, up_cot, preferred_element_type=jnp.float32)
               + decay[1] * (1.0 - mask_up.astype(jnp.float32)) * up_weight.astype(jnp.float32)).astype(jnp.bfloat16)
    down_grad = (jnp.dot(hidden.T, cotangent, preferred_element_type=jnp.float32)
                 + decay[2] * (1.0 - mask_down.astype(jnp.float32)) * down_weight.astype(jnp.float32)).astype(jnp.bfloat16)
    return layer_out, input_grad, gate_grad, up_grad, down_grad
```

```python
import functools

import jax
import jax.numpy as jnp
from jax import lax
from jax.experimental import pallas as pl
from jax.experimental.pallas import tpu as pltpu
from jax.sharding import PartitionSpec as P

BLK = 128
N_CHUNKS = 4
NT = (((1,), (1,)), ((), ()))
TN = (((0,), (0,)), ((), ()))
F32 = jnp.float32
BF16 = jnp.bfloat16
PARAMS = pltpu.CompilerParams(vmem_limit_bytes=56 * 1024 * 1024)


def kept_blocks(block_lists, block_counts):
    rows = block_lists[:, :, 0, :]
    counts = block_counts[:, :, 0]
    position = jnp.arange(rows.shape[2], dtype=jnp.int32)
    live = position[None, None, :] < counts[:, :, None]
    hits = (rows[..., None] == position) & live[..., None]
    return jnp.any(hits, axis=2)


def masked_rows(weight, mask, out):
    for r in range(mask.shape[0]):
        rows = pl.ds(r * BLK, BLK)
        out[rows, :] = weight[rows, :] * mask[r : r + 1, :]


def forward_body(both, gate_w, up_w, down_w, gate_m, up_m, down_m, out, cols, rows):
    width = gate_w.shape[0]
    tile = gate_w.shape[1]
    acts = both[:, :width]
    cot = both[:, width:]
    masked_rows(gate_w, gate_m, cols)
    out[:, :tile] = jnp.dot(acts, cols[...], preferred_element_type=F32).astype(BF16)
    masked_rows(up_w, up_m, cols)
    out[:, tile : 2 * tile] = jnp.dot(acts, cols[...], preferred_element_type=F32).astype(BF16)
    masked_rows(down_w, down_m.at[0], rows)
    out[:, 2 * tile :] = lax.dot_general(cot, rows[...], NT, preferred_element_type=F32).astype(BF16)


def act_body(sums, out):
    tile = sums.shape[1] // 3
    gate = sums[:, :tile].astype(F32)
    up = sums[:, tile : 2 * tile].astype(F32)
    grad_hidden = sums[:, 2 * tile :].astype(F32)
    sigma = 1.0 / (1.0 + jnp.exp(-gate))
    silu = gate * sigma
    out[:, :tile] = (silu * up).astype(BF16)
    out[:, tile : 2 * tile] = (grad_hidden * up * sigma * (1.0 + gate * (1.0 - sigma))).astype(BF16)
    out[:, 2 * tile :] = (grad_hidden * silu).astype(BF16)


def weight_grad(lhs_t, rhs, weight, mask, decay, out):
    step = 2 * BLK if lhs_t.shape[0] % (2 * BLK) == 0 else BLK
    for r in range(0, lhs_t.shape[0], step):
        product = jnp.dot(lhs_t[r : r + step, :], rhs, preferred_element_type=F32)
        for q in range(0, step, BLK):
            row = (r + q) // BLK
            factor = decay * (1.0 - mask[row : row + 1, :].astype(F32))
            rows = pl.ds(r + q, BLK)
            out[rows, :] = (product[q : q + BLK] + factor * weight[rows, :].astype(F32)).astype(BF16)


def backward_body(first, last, *refs):
    (decay, both, acts_t, joined, gate_w, up_w, down_w, gate_m, up_m, down_m) = refs[:10]
    refs = refs[10:]
    if not first:
        prev, refs = refs[0], refs[4:]
    gate_g, up_g, down_g, sums, cols, rows, acc = refs
    width, tile = gate_w.shape
    step = pl.program_id(0)
    hidden = joined[:, :tile]
    gate_cot = joined[:, tile : 2 * tile]
    up_cot = joined[:, 2 * tile :]

    @pl.when(step == 0)
    def _():
        acc[...] = jnp.zeros_like(acc) if first else prev[...]

    masked_rows(down_w, down_m.at[0], rows)
    acc[:, :width] += jnp.dot(hidden, rows[...], preferred_element_type=F32)
    masked_rows(gate_w, gate_m, cols)
    acc[:, width:] += lax.dot_general(gate_cot, cols[...], NT, preferred_element_type=F32)
    masked_rows(up_w, up_m, cols)
    acc[:, width:] += lax.dot_general(up_cot, cols[...], NT, preferred_element_type=F32)
    weight_grad(acts_t, gate_cot, gate_w, gate_m, decay[0], gate_g)
    weight_grad(acts_t, up_cot, up_w, up_m, decay[1], up_g)
    hidden_t = hidden.T
    weight_grad(hidden_t, both[:, width:], down_w, down_m.at[0], decay[2], down_g)

    @pl.when(step == pl.num_programs(0) - 1)
    def _():
        sums[...] = acc[...].astype(sums.dtype)


def whole(shape):
    return pl.BlockSpec(shape, lambda i: (0,) * len(shape))


def weight_specs(width, tile, start):
    per_tile = tile // BLK
    col = lambda i: (0, start + i)
    row = lambda i: (start + i, 0)
    w = [pl.BlockSpec((width, tile), col)] * 2 + [pl.BlockSpec((tile, width), row)]
    m = [pl.BlockSpec((width // BLK, tile), col)] * 2 + [
        pl.BlockSpec((1, per_tile, width), lambda i: (start + i, 0, 0))
    ]
    return w, m


def shards(acts, cotangent, gate_weight, up_weight, down_weight, block_lists, block_counts, decay):
    width, hid = gate_weight.shape
    blocks = hid // BLK
    tile = 2 * BLK if blocks % 2 == 0 else BLK
    n_tiles = hid // tile
    chunks = min(N_CHUNKS, n_tiles)
    edges = [n_tiles * c // chunks for c in range(chunks + 1)]
    both = lax.all_gather(jnp.concatenate([acts, cotangent], axis=1), "wide", axis=0, tiled=True)
    tokens = both.shape[0]
    kept = kept_blocks(block_lists, block_counts).astype(BF16)
    gate_m = jnp.repeat(kept[0].T, BLK, 1)
    up_m = jnp.repeat(kept[1].T, BLK, 1)
    down_m = jnp.repeat(kept[2], BLK, 1).reshape(n_tiles, tile // BLK, width)
    acts_t = both[:, :width].T
    scratch = [pltpu.VMEM((width, tile), BF16), pltpu.VMEM((tile, width), BF16)]
    operands = (gate_weight, up_weight, down_weight, gate_m, up_m, down_m)
    flops = 2 * tokens * width * tile * 3
    moved = 3 * width * tile * 2

    joined = []
    for c in range(chunks):
        start, count = edges[c], edges[c + 1] - edges[c]
        w_specs, m_specs = weight_specs(width, tile, start)
        part = pl.pallas_call(
            forward_body,
            grid=(count,),
            in_specs=[whole((tokens, 2 * width))] + w_specs + m_specs,
            out_specs=pl.BlockSpec((tokens, 3 * tile), lambda i: (0, i)),
            out_shape=jax.ShapeDtypeStruct((tokens, 3 * tile * count), BF16),
            scratch_shapes=scratch,
            compiler_params=PARAMS,
            cost_estimate=pl.CostEstimate(flops=flops * count, bytes_accessed=moved * count, transcendentals=0),
            name="forward",
        )(both, *operands)
        sums = lax.psum_scatter(part, "tok", scatter_dimension=0, tiled=True)
        mine = sums.shape[0]
        spec = pl.BlockSpec((mine, 3 * tile), lambda i: (0, i))
        active = pl.pallas_call(
            act_body,
            grid=(count,),
            in_specs=[spec],
            out_specs=spec,
            out_shape=jax.ShapeDtypeStruct(sums.shape, BF16),
            name="activate",
        )(sums)
        joined.append(lax.all_gather(active, "tok", axis=0, tiled=True))

    state = ()
    for c in range(chunks):
        start, count = edges[c], edges[c + 1] - edges[c]
        first, last = c == 0, c == chunks - 1
        w_specs, m_specs = weight_specs(width, tile, start)
        aliases = {} if first else {11: 0, 12: 1, 13: 2}
        extra = [] if first else [whole((tokens, 2 * width))] + [pl.BlockSpec(memory_space=pl.ANY)] * 3
        gate_g, up_g, down_g, sums = pl.pallas_call(
            functools.partial(backward_body, first, last),
            grid=(count,),
            in_specs=[
                pl.BlockSpec(memory_space=pltpu.SMEM),
                whole((tokens, 2 * width)),
                whole((width, tokens)),
                pl.BlockSpec((tokens, 3 * tile), lambda i: (0, i)),
            ]
            + w_specs
            + m_specs
            + extra,
            out_specs=w_specs + [whole((tokens, 2 * width))],
            out_shape=[
                jax.ShapeDtypeStruct(gate_weight.shape, BF16),
                jax.ShapeDtypeStruct(up_weight.shape, BF16),
                jax.ShapeDtypeStruct(down_weight.shape, BF16),
                jax.ShapeDtypeStruct((tokens, 2 * width), BF16 if last else F32),
            ],
            scratch_shapes=scratch + [pltpu.VMEM((tokens, 2 * width), F32)],
            input_output_aliases=aliases,
            compiler_params=PARAMS,
            cost_estimate=pl.CostEstimate(flops=2 * flops * count, bytes_accessed=2 * moved * count, transcendentals=0),
            name="backward",
        )(decay, both, acts_t, joined[c], *operands, *state)
        state = (sums, gate_g, up_g, down_g)
    out = lax.psum_scatter(state[0], "wide", scatter_dimension=0, tiled=True)
    return (out[:, :width], out[:, width:], gate_g, up_g, down_g)


def solution(mesh):
    placed = (
        P(("groups", "wide"), "tok"),
        P(("groups", "wide"), "tok"),
        P("tok", "wide"),
        P("tok", "wide"),
        P("wide", "tok"),
        P(None, "wide", "tok", None),
        P(None, "wide", "tok"),
        P(),
    )
    return jax.shard_map(
        shards,
        mesh=mesh,
        in_specs=placed,
        out_specs=(
            P(("groups", "wide"), "tok"),
            P(("groups", "wide"), "tok"),
            P(("groups", "tok"), "wide"),
            P(("groups", "tok"), "wide"),
            P(("groups", "wide"), "tok"),
        ),
        check_vma=False,
    )
```

```python
import functools

import jax
import jax.numpy as jnp
from jax import lax
from jax.experimental import pallas as pl
from jax.experimental.pallas import tpu as pltpu
from jax.sharding import PartitionSpec as P

BLK = 128
NT = (((1,), (1,)), ((), ()))
NN = (((1,), (0,)), ((), ()))
FORWARD_LAG = 2
OUT_LAG = 5
F32 = jnp.float32
BF16 = jnp.bfloat16
PARAMS = pltpu.CompilerParams(vmem_limit_bytes=56 * 1024 * 1024)


def kept_blocks(block_lists, block_counts):
    rows = block_lists[:, :, 0, :]
    counts = block_counts[:, :, 0]
    position = jnp.arange(rows.shape[2], dtype=jnp.int32)
    live = position[None, None, :] < counts[:, :, None]
    hits = (rows[..., None] == position) & live[..., None]
    return jnp.any(hits, axis=2)


def masked_rows(weight, mask, out):
    for r in range(mask.shape[0]):
        rows = pl.ds(r * BLK, BLK)
        out[rows, :] = weight[rows, :] * mask[r : r + 1, :]


def line_body(n, n_tiles, both, gate_w, up_w, down_w, gate_m, up_m, down_m, out, cols, rows, total,
              mine, from_left, from_right, result, sent_in, sent_left, sent_right, got_left, got_right, got_result):
    i = pl.program_id(0)
    z = lax.axis_index("tok")
    width, tile = gate_w.shape

    def home(t):
        return n // 2 - 1 + t % 2

    def inward(t, right):
        side, sem = (from_left, got_left) if right else (from_right, got_right)
        return pltpu.make_async_remote_copy(
            mine.at[t], side.at[t], sent_in.at[t], sem.at[t],
            device_id={"tok": z + 1 if right else z - 1}, device_id_type=pl.DeviceIdType.MESH)

    def outward(t, right):
        return pltpu.make_async_remote_copy(
            result.at[t], result.at[t], (sent_right if right else sent_left).at[t], got_result.at[t],
            device_id={"tok": z + 1 if right else z - 1}, device_id_type=pl.DeviceIdType.MESH)

    @pl.when(i == 0)
    def _():
        barrier = pltpu.get_barrier_semaphore()

        @pl.when(z > 0)
        def _():
            pl.semaphore_signal(barrier, inc=1, device_id={"tok": z - 1}, device_id_type=pl.DeviceIdType.MESH)

        @pl.when(z < n - 1)
        def _():
            pl.semaphore_signal(barrier, inc=1, device_id={"tok": z + 1}, device_id_type=pl.DeviceIdType.MESH)

        @pl.when((z > 0) & (z < n - 1))
        def _():
            pl.semaphore_wait(barrier, 2)

        @pl.when((z == 0) | (z == n - 1))
        def _():
            pl.semaphore_wait(barrier, 1)

    def bf16_sum(lhs, rhs, dims):
        return lax.dot_general(lhs, rhs, dims, preferred_element_type=F32).astype(BF16).astype(F32)

    @pl.when(i < n_tiles)
    def _():
        h = home(i)
        acts = both[:, :width]
        masked_rows(gate_w, gate_m, cols)
        total[:, :tile] = bf16_sum(acts, cols[...], NN)
        masked_rows(up_w, up_m, cols)
        total[:, tile : 2 * tile] = bf16_sum(acts, cols[...], NN)
        masked_rows(down_w, down_m.at[0], rows)
        total[:, 2 * tile :] = bf16_sum(both[:, width:], rows[...], NT)

        @pl.when((z > 0) & (z <= h))
        def _():
            inward(i, True).wait_recv()
            total[...] += from_left[i].astype(F32)

        @pl.when((z < n - 1) & (z >= h))
        def _():
            inward(i, False).wait_recv()
            total[...] += from_right[i].astype(F32)

        @pl.when(z != h)
        def _():
            mine[i] = total[...].astype(BF16)

        @pl.when(z < h)
        def _():
            inward(i, True).start()

        @pl.when(z > h)
        def _():
            inward(i, False).start()

        @pl.when(z == h)
        def _():
            gate = total[:, :tile]
            up = total[:, tile : 2 * tile]
            grad_hidden = total[:, 2 * tile :]
            sigma = 1.0 / (1.0 + jnp.exp(-gate))
            silu = gate * sigma
            result[i, :, :tile] = (silu * up).astype(BF16)
            result[i, :, tile : 2 * tile] = (grad_hidden * up * sigma * (1.0 + gate * (1.0 - sigma))).astype(BF16)
            result[i, :, 2 * tile :] = (grad_hidden * silu).astype(BF16)

            @pl.when(z > 0)
            def _():
                outward(i, False).start()

            @pl.when(z < n - 1)
            def _():
                outward(i, True).start()

    j = i - FORWARD_LAG

    @pl.when((j >= 0) & (j < n_tiles) & (z > 0) & (z < n - 1))
    def _():
        h = home(j)

        @pl.when(z < h)
        def _():
            outward(j, False).wait_recv()
            outward(j, False).start()

        @pl.when(z > h)
        def _():
            outward(j, True).wait_recv()
            outward(j, True).start()

    k = i - OUT_LAG

    @pl.when(k >= 0)
    def _():
        @pl.when(((z == 0) | (z == n - 1)) & (z != home(k)))
        def _():
            outward(k, False).wait_recv()

        out[...] = result[k]

    @pl.when(i == n_tiles + OUT_LAG - 1)
    def _():
        def drain(t, carry):
            h = home(t)

            @pl.when(z != h)
            def _():
                inward(t, True).wait_send()

            @pl.when((z <= h) & (z > 0))
            def _():
                outward(t, False).wait_send()

            @pl.when((z >= h) & (z < n - 1))
            def _():
                outward(t, True).wait_send()

            return carry

        lax.fori_loop(0, n_tiles, drain, 0)


def scatter_body(n, part, layer, grad, landed, sent, got):
    me = lax.axis_index("wide")
    rows, width = layer.shape
    barrier = pltpu.get_barrier_semaphore()
    for k in range(1, n):
        pl.semaphore_signal(
            barrier, inc=1, device_id={"wide": lax.rem(me + k, n)}, device_id_type=pl.DeviceIdType.MESH)
    pl.semaphore_wait(barrier, n - 1)
    copies = []
    for k in range(1, n):
        peer = lax.rem(me + k, n)
        copy = pltpu.make_async_remote_copy(
            part.at[pl.ds(pl.multiple_of(peer * rows, rows), rows)], landed.at[k], sent.at[k], got.at[k],
            device_id={"wide": peer}, device_id_type=pl.DeviceIdType.MESH)
        copy.start()
        copies.append(copy)
    acc = part[pl.ds(pl.multiple_of(me * rows, rows), rows), :].astype(F32)
    for k in range(1, n):
        copies[k - 1].wait_recv()
        acc += landed[k].astype(F32)
    layer[...] = acc[:, :width].astype(BF16)
    grad[...] = acc[:, width:].astype(BF16)
    for copy in copies:
        copy.wait_send()


def weight_grad(lhs_t, rhs, weight, mask, decay, out):
    step = 2 * BLK if lhs_t.shape[0] % (2 * BLK) == 0 else BLK
    for r in range(0, lhs_t.shape[0], step):
        product = jnp.dot(lhs_t[r : r + step, :], rhs, preferred_element_type=F32)
        for q in range(0, step, BLK):
            row = (r + q) // BLK
            factor = decay * (1.0 - mask[row : row + 1, :].astype(F32))
            rows = pl.ds(r + q, BLK)
            out[rows, :] = (product[q : q + BLK] + factor * weight[rows, :].astype(F32)).astype(BF16)


def backward_body(decay, both, acts_t, joined, gate_w, up_w, down_w, gate_m, up_m, down_m,
                  gate_g, up_g, down_g, sums, cols, rows, acc):
    width, tile = gate_w.shape
    step = pl.program_id(0)
    hidden = joined[:, :tile]
    gate_cot = joined[:, tile : 2 * tile]
    up_cot = joined[:, 2 * tile :]

    @pl.when(step == 0)
    def _():
        acc[...] = jnp.zeros_like(acc)

    masked_rows(down_w, down_m.at[0], rows)
    acc[:, :width] += jnp.dot(hidden, rows[...], preferred_element_type=F32)
    masked_rows(gate_w, gate_m, cols)
    acc[:, width:] += lax.dot_general(gate_cot, cols[...], NT, preferred_element_type=F32)
    masked_rows(up_w, up_m, cols)
    acc[:, width:] += lax.dot_general(up_cot, cols[...], NT, preferred_element_type=F32)
    weight_grad(acts_t, gate_cot, gate_w, gate_m, decay[0], gate_g)
    weight_grad(acts_t, up_cot, up_w, up_m, decay[1], up_g)
    hidden_t = hidden.T
    weight_grad(hidden_t, both[:, width:], down_w, down_m.at[0], decay[2], down_g)

    @pl.when(step == pl.num_programs(0) - 1)
    def _():
        sums[...] = acc[...].astype(sums.dtype)


def whole(shape):
    return pl.BlockSpec(shape, lambda i: (0,) * len(shape))


def weight_specs(width, tile, at):
    per_tile = tile // BLK
    col = lambda i: (0, at(i))
    row = lambda i: (at(i), 0)
    w = [pl.BlockSpec((width, tile), col)] * 2 + [pl.BlockSpec((tile, width), row)]
    m = [pl.BlockSpec((width // BLK, tile), col)] * 2 + [
        pl.BlockSpec((1, per_tile, width), lambda i: (at(i), 0, 0))
    ]
    return w, m


def shards(acts, cotangent, gate_weight, up_weight, down_weight, block_lists, block_counts, decay):
    width, hid = gate_weight.shape
    blocks = hid // BLK
    tile = 2 * BLK if blocks % 2 == 0 else BLK
    n_tiles = hid // tile
    both = lax.all_gather(jnp.concatenate([acts, cotangent], axis=1), "wide", axis=0, tiled=True)
    tokens = both.shape[0]
    kept = kept_blocks(block_lists, block_counts).astype(BF16)
    gate_m = jnp.repeat(kept[0].T, BLK, 1)
    up_m = jnp.repeat(kept[1].T, BLK, 1)
    down_m = jnp.repeat(kept[2], BLK, 1).reshape(n_tiles, tile // BLK, width)
    acts_t = both[:, :width].T
    scratch = [pltpu.VMEM((width, tile), BF16), pltpu.VMEM((tile, width), BF16)]
    operands = (gate_weight, up_weight, down_weight, gate_m, up_m, down_m)

    n_tok, n_wide = lax.axis_size("tok"), lax.axis_size("wide")
    at = lambda i: jnp.minimum(i, n_tiles - 1)
    w_specs, m_specs = weight_specs(width, tile, at)
    stage = pltpu.VMEM((n_tiles, tokens, 3 * tile), BF16)
    joined = pl.pallas_call(
        functools.partial(line_body, n_tok, n_tiles),
        grid=(n_tiles + OUT_LAG,),
        in_specs=[whole((tokens, 2 * width))] + w_specs + m_specs,
        out_specs=pl.BlockSpec((tokens, 3 * tile), lambda i: (0, jnp.maximum(i - OUT_LAG, 0))),
        out_shape=jax.ShapeDtypeStruct((tokens, 3 * tile * n_tiles), BF16),
        scratch_shapes=scratch
        + [pltpu.VMEM((tokens, 3 * tile), F32), stage, stage, stage, stage]
        + [pltpu.SemaphoreType.DMA((n_tiles,))] * 6,
        compiler_params=pltpu.CompilerParams(
            vmem_limit_bytes=56 * 1024 * 1024, collective_id=1, has_side_effects=True),
        name="forward_line",
    )(both, *operands)

    w_specs, m_specs = weight_specs(width, tile, lambda i: i)
    gate_g, up_g, down_g, sums = pl.pallas_call(
        backward_body,
        grid=(n_tiles,),
        in_specs=[
            pl.BlockSpec(memory_space=pltpu.SMEM),
            whole((tokens, 2 * width)),
            whole((width, tokens)),
            pl.BlockSpec((tokens, 3 * tile), lambda i: (0, i)),
        ]
        + w_specs
        + m_specs,
        out_specs=w_specs + [whole((tokens, 2 * width))],
        out_shape=[
            jax.ShapeDtypeStruct(gate_weight.shape, BF16),
            jax.ShapeDtypeStruct(up_weight.shape, BF16),
            jax.ShapeDtypeStruct(down_weight.shape, BF16),
            jax.ShapeDtypeStruct((tokens, 2 * width), BF16),
        ],
        scratch_shapes=scratch + [pltpu.VMEM((tokens, 2 * width), F32)],
        compiler_params=PARAMS,
        name="backward",
    )(decay, both, acts_t, joined, *operands)
    mine = tokens // n_wide
    vmem = pl.BlockSpec(memory_space=pltpu.VMEM)
    layer, grad = pl.pallas_call(
        functools.partial(scatter_body, n_wide),
        in_specs=[vmem],
        out_specs=[vmem, vmem],
        out_shape=[jax.ShapeDtypeStruct((mine, width), BF16)] * 2,
        scratch_shapes=[pltpu.VMEM((n_wide, mine, 2 * width), BF16)] + [pltpu.SemaphoreType.DMA((n_wide,))] * 2,
        compiler_params=pltpu.CompilerParams(
            vmem_limit_bytes=32 * 1024 * 1024, collective_id=2, has_side_effects=True),
        name="scatter",
    )(sums)
    return (layer, grad, gate_g, up_g, down_g)


def solution(mesh):
    placed = (
        P(("groups", "wide"), "tok"),
        P(("groups", "wide"), "tok"),
        P("tok", "wide"),
        P("tok", "wide"),
        P("wide", "tok"),
        P(None, "wide", "tok", None),
        P(None, "wide", "tok"),
        P(),
    )
    return jax.shard_map(
        shards,
        mesh=mesh,
        in_specs=placed,
        out_specs=(
            P(("groups", "wide"), "tok"),
            P(("groups", "wide"), "tok"),
            P(("groups", "tok"), "wide"),
            P(("groups", "tok"), "wide"),
            P(("groups", "wide"), "tok"),
        ),
        check_vma=False,
    )
```
